32 devices in a mesh: row: 16 (over z, x, core), col: 2 (over y).
Axes of the slice: x: 2, y: 2, z: 4, core: 2. Of those that a mesh axis runs over, the one named last changes fastest.
Arguments:
- dist_first: bfloat16 [32768, 32768], P('row', 'col'), may hold values from -0.34 to 0.34
- coupling: bfloat16 [32768, 256], P('row', 'col'), may hold values from 0.099609375 to 1
- dist_second: bfloat16 [256, 512], P(None, 'col'), may hold values from -12 to 12
- row_potential: float32 [32768], P('row'), may hold values from -150 to 120
- column_cost: float32 [512], P('col'), may hold values from -300 to 20
- column_mass: float32 [512], P('col'), may hold values from 0.5 to 2
Outputs:
- transport: bfloat16 [32768, 512], P('row', 'col')
- potential: float32 [512], P('col')
The draws below stay inside these ranges and needn't reach their ends.
All inputs are finite; a program needn't handle non-finite values.
Results may differ from the reference program's by a relative error of at most 0.0051.
Values may be sent and summed in bfloat16 or wider, within the bound.
A program may use at most 128 MiB of HBM per device.

```python
import math
import jax
import jax.numpy as jnp

N = 32768
Q = 512
K = 256


def draw_dist_first(key, part):
    noise_key = jax.random.fold_in(jax.random.fold_in(key, 11), 0)
    values = jax.random.truncated_normal(noise_key, -6.0, 6.0, (N, N), jnp.float32) / math.sqrt(N)
    return jnp.clip(values, -0.34, 0.34).astype(jnp.bfloat16)


def draw_dist_second(key, part):
    noise_key = jax.random.fold_in(jax.random.fold_in(key, 53), 0)
    values = jax.random.truncated_normal(noise_key, -6.0, 6.0, (K, Q), jnp.float32) / math.sqrt(4.0 * K)
    return jnp.clip(values, -12.0, 12.0).astype(jnp.bfloat16)


def draw_row_potential(key, part):
    noise_key = jax.random.fold_in(jax.random.fold_in(key, 23), 0)
    ramp = jnp.arange(N, dtype=jnp.float32) / N
    values = 0.5 * jax.random.normal(noise_key, (N,), jnp.float32) + 1.2 * ramp
    return values


def draw_column_cost(key, part):
    noise_key = jax.random.fold_in(jax.random.fold_in(key, 37), 0)
    values = 0.5 * jax.random.truncated_normal(noise_key, -6.0, 6.0, (Q,), jnp.float32)
    return values


def level_of(key, extent, cuts, smallest, top_value):
    level = 1.0
    for axis_at, blocks in cuts:
        steps = jax.random.uniform(jax.random.fold_in(jax.random.fold_in(key, 6), axis_at), (blocks,), jnp.float32, smallest / len(cuts), top_value / len(cuts))
        level = level * jnp.repeat(jnp.exp(steps), extent[axis_at] // blocks).reshape((-1,) + (1,) * (len(extent) - 1 - axis_at))
    return level


def setup_inputs(seed: int = 0) -> dict:
    arg_keys = jax.random.split(jax.random.key(seed), 7)
    return {
        "dist_first": draw_dist_first(jax.random.fold_in(arg_keys[6], 71), 0),
        "coupling": jnp.clip(jnp.exp(math.log(1.0) - 2.306499 * jax.random.uniform(arg_keys[1], (N, K), jnp.float32) ** level_of(arg_keys[1], (N, K), ((0, 16), (1, 2)), -0.2, 0.2)), 0.099609375, 1.0).astype(jnp.bfloat16),
        "dist_second": draw_dist_second(jax.random.fold_in(arg_keys[6], 71), 0),
        "row_potential": draw_row_potential(jax.random.fold_in(arg_keys[6], 71), 0),
        "column_cost": draw_column_cost(jax.random.fold_in(arg_keys[6], 71), 0),
        "column_mass": jnp.clip(jnp.exp(math.log(2.0) - 1.3862944 * jax.random.uniform(arg_keys[5], (Q,), jnp.float32) ** level_of(arg_keys[5], (Q,), ((0, 2),), -0.2, 0.2)), 0.5, 2.0),
    }


def reference(dist_first, coupling, dist_second, row_potential, column_cost, column_mass):
    product = jnp.dot(coupling, dist_second, preferred_element_type=jnp.float32).astype(jnp.bfloat16)
    gradient = jnp.dot(dist_first, product, preferred_element_type=jnp.float32)
    scores = row_potential[:, None] + 2.0 * gradient - column_cost[None, :]
    highest = jnp.max(scores, axis=0)
    weights = jnp.exp(scores - highest[None, :])
    column_sum = jnp.sum(weights, axis=0)
    potential = jnp.log(column_mass) - highest - jnp.log(column_sum)
    transport = (weights * (N * column_mass / column_sum)[None, :]).astype(jnp.bfloat16)
    return transport, potential
```

```python
import functools

import jax
import jax.numpy as jnp
from jax import lax
from jax.experimental import pallas as pl
from jax.experimental.pallas import tpu as pltpu
from jax.sharding import PartitionSpec as P

LEVELS = 4
SUBS = 4
CHUNKS = 8
SEND = jnp.float32
MESH = pl.DeviceIdType.MESH


def kernel(
    n_rows, width, total,
    dist_ref, coup_ref, second_ref, rowpot_ref, cost_ref, mass_ref,
    trans_ref, pot_ref,
    call, sfull, dbuf, pbuf, acc, rpb, exs, exr, stat, cmax,
    d_sem, loc_sem, y_send, z_send, x_send, c_send, recv,
    s_send, s_recv, e_send, e_recv, st_send, st_recv,
):
    m = coup_ref.shape[0]
    mp = m // SUBS
    mc = m // CHUNKS
    nb = n_rows // (2 * LEVELS)
    half = second_ref.shape[1]
    kc = coup_ref.shape[1]
    n_sub = 2 * nb
    steps = 2 * SUBS

    r = lax.axis_index("row")
    y = lax.axis_index("col")
    core = lax.rem(r, 2)
    q = lax.div(r, 2)
    b = lax.rem(q, nb)
    a = lax.div(q, nb)

    def flip(v, col):
        return v + col * (LEVELS - 1 - 2 * v)

    at = flip(a, y)

    def row_of(level, bb, kk):
        return (flip(level, y) * nb + bb) * 2 + kk

    def slot(level, bb, kk, col):
        return ((level + col * (1 - 2 * level)) * nb + bb) * 2 + kk

    def region(level, bb, kk, kind, p, col):
        start = pl.multiple_of(slot(level, bb, kk, col) * m + p * mp, mp)
        return call.at[pl.ds(start, mp), pl.ds(pl.multiple_of(kind * kc, kc), kc)]

    partner = (r, 1 - y)
    first = jnp.where(at == 0, 0, 1)

    def order(j):
        late = lax.div(j, SUBS)
        level = first + late * (1 - 2 * first)
        return level, j - late * SUBS

    def fetch(j, start):
        level, p = order(j)
        buf = lax.rem(j, 2)
        for i in range(n_sub):
            col0 = pl.multiple_of(slot(level, i // 2, i % 2, y) * m + p * mp, mp)
            cp = pltpu.make_async_copy(
                dist_ref.at[:, pl.ds(col0, mp)],
                dbuf.at[buf, :, pl.ds(i * mp, mp)],
                d_sem.at[buf, i],
            )
            if start:
                cp.start()
            else:
                cp.wait()

    fetch(0, True)

    barrier = pltpu.get_barrier_semaphore()

    @pl.loop(1, n_rows)
    def _(j):
        pl.semaphore_signal(
            barrier, inc=1, device_id=(lax.rem(r + j, n_rows), y), device_id_type=MESH
        )

    pl.semaphore_signal(barrier, inc=1, device_id=partner, device_id_type=MESH)
    pl.semaphore_wait(barrier, n_rows)

    second_copy = pltpu.make_async_remote_copy(
        src_ref=second_ref, dst_ref=sfull.at[:, pl.ds(half, half)],
        send_sem=s_send, recv_sem=s_recv, device_id=partner, device_id_type=MESH,
    )
    second_copy.start()
    second_local = pltpu.make_async_copy(
        second_ref, sfull.at[:, pl.ds(0, half)], loc_sem.at[0]
    )
    second_local.start()

    def y_copy(p):
        return pltpu.make_async_remote_copy(
            src_ref=coup_ref.at[pl.ds(p * mp, mp), :],
            dst_ref=region(LEVELS - 1 - at, b, core, y, p, 1 - y),
            send_sem=y_send.at[p],
            recv_sem=recv.at[LEVELS - 1 - at, b, core, y, p],
            device_id=partner, device_id_type=MESH,
        )

    @pl.when(at >= 2)
    def _():
        for p in range(SUBS):
            y_copy(p).start()

    def own_copy():
        start = pl.multiple_of(slot(at, b, core, y) * m, m)
        return pltpu.make_async_copy(
            coup_ref,
            call.at[pl.ds(start, m), pl.ds(pl.multiple_of(y * kc, kc), kc)],
            loc_sem.at[1],
        )

    @pl.when(at < 2)
    def _():
        own_copy().start()
        own_copy().wait()

    second_local.wait()

    def copy(level, bb, kk, kind, p, send_sem, device):
        ref = region(level, bb, kk, kind, p, y)
        return pltpu.make_async_remote_copy(
            src_ref=ref, dst_ref=ref, send_sem=send_sem,
            recv_sem=recv.at[level, bb, kk, kind, p],
            device_id=device, device_id_type=MESH,
        )

    def up_copy(level, kind, p):
        dev = (row_of(jnp.minimum(at + 1, LEVELS - 1), b, core), y)
        return copy(level, b, core, kind, p, z_send.at[0, level, kind, p], dev)

    def down_copy(level, kind, p):
        dev = (row_of(jnp.maximum(at - 1, 0), b, core), y)
        return copy(level, b, core, kind, p, z_send.at[1, level, kind, p], dev)

    def side_copy(j, level, kind, p):
        dev = (row_of(at, lax.rem(b + j, nb), core), y)
        return copy(level, b, core, kind, p, x_send.at[j, level, kind, p], dev)

    def core_copy(bb, level, kind, p):
        dev = (row_of(at, b, 1 - core), y)
        return copy(level, bb, core, kind, p, c_send.at[bb, level, kind, p], dev)

    def wait_piece(level, bb, kk, kind, p):
        dev = (row_of(at, b, 1 - core), y)
        copy(level, bb, kk, kind, p, c_send.at[bb, level, kind, p], dev).wait_recv()

    def sends_up(level):
        return jnp.logical_or(
            jnp.logical_and(at == 0, level == 0), jnp.logical_or(at == 1, at == 2)
        )

    def sends_down(level):
        return jnp.logical_and(at == 1, level == 1)

    def forward(level, p):
        for late in range(2):
            kind = y + late * (1 - 2 * y)
            if late == 0:
                @pl.when(level != at)
                def _():
                    wait_piece(level, b, core, kind, p)
            else:
                wait_piece(level, b, core, kind, p)

            @pl.when(sends_up(level))
            def _():
                up_copy(level, kind, p).start()

            @pl.when(sends_down(level))
            def _():
                down_copy(level, kind, p).start()

            for j in range(1, nb):
                side_copy(j, level, kind, p).start()
            core_copy(b, level, kind, p).start()

    def cross(level, p):
        for j in range(1, nb):
            bb = lax.rem(b + j, nb)
            for kind in range(2):
                wait_piece(level, bb, core, kind, p)
                core_copy(bb, level, kind, p).start()

    def gathered(level, p):
        for j in range(nb):
            bb = lax.rem(b + j, nb)
            for kind in range(2):
                wait_piece(level, bb, 1 - core, kind, p)

    def make_product(level, p):
        for i in range(n_sub):
            start = pl.multiple_of(slot(level, i // 2, i % 2, y) * m + p * mp, mp)
            pbuf[i * mp:(i + 1) * mp, :] = jnp.dot(
                call[pl.ds(start, mp), :], sfull[...], preferred_element_type=jnp.float32
            ).astype(jnp.bfloat16)

    forward(*order(0))

    for i in range(m // 128):
        line = jnp.broadcast_to(rowpot_ref[i:i + 1, :], (128, 128))
        rpb[i * 128:(i + 1) * 128, :] = line.T

    second_copy.wait_recv()

    def ex_copy(c):
        rows = pl.ds(pl.multiple_of(c * mc, mc), mc)
        return pltpu.make_async_remote_copy(
            src_ref=exs.at[rows, :], dst_ref=exr.at[rows, :],
            send_sem=e_send.at[c], recv_sem=e_recv.at[c],
            device_id=partner, device_id_type=MESH,
        )

    @pl.loop(0, steps)
    def _(j):
        level, p = order(j)

        @pl.when(j + 1 < steps)
        def _():
            forward(*order(j + 1))
            fetch(j + 1, True)

        cross(level, p)
        gathered(level, p)
        make_product(level, p)
        fetch(j, False)
        buf = lax.rem(j, 2)

        @pl.loop(0, CHUNKS)
        def _(c):
            rows = pl.ds(pl.multiple_of(c * mc, mc), mc)
            value = jnp.dot(
                dbuf[buf, rows, :], pbuf[...], preferred_element_type=jnp.float32
            )

            @pl.when(j == 0)
            def _():
                acc[rows, :] = value

            @pl.when(jnp.logical_and(j > 0, j < steps - 1))
            def _():
                acc[rows, :] += value

            @pl.when(j == steps - 1)
            def _():
                done = acc[rows, :] + value
                acc[rows, 0:half] = done[:, 0:half]
                exs[rows, :] = done[:, half:].astype(SEND)
                ex_copy(c).start()

    @pl.loop(0, CHUNKS)
    def _(c):
        ex_copy(c).wait()
        rows = pl.ds(pl.multiple_of(c * mc, mc), mc)
        gradient = acc[rows, 0:half] + exr[rows, :].astype(jnp.float32)
        pot = jnp.concatenate([rpb[rows, :]] * (half // 128), axis=1)
        scores = pot + 2.0 * gradient - cost_ref[...]
        high = jnp.max(scores, axis=0, keepdims=True)
        weights = jnp.exp(scores - high)
        acc[rows, 0:half] = weights
        cmax[c, 0:1, :] = high
        cmax[c, 1:2, :] = jnp.sum(weights, axis=0, keepdims=True)

    highs = cmax[:, 0, :]
    high = jnp.max(highs, axis=0, keepdims=True)
    sums = jnp.sum(cmax[:, 1, :] * jnp.exp(highs - high), axis=0, keepdims=True)
    stat[r, 0:1, :] = high
    stat[r, 1:2, :] = sums

    def stat_copy(j, src):
        return pltpu.make_async_remote_copy(
            src_ref=stat.at[src], dst_ref=stat.at[src],
            send_sem=st_send.at[j], recv_sem=st_recv.at[src],
            device_id=(lax.rem(r + j, n_rows), y), device_id_type=MESH,
        )

    @pl.loop(1, n_rows)
    def _(j):
        stat_copy(j, r).start()

    second_copy.wait_send()

    @pl.when(at >= 2)
    def _():
        for p in range(SUBS):
            y_copy(p).wait_send()

    @pl.loop(0, steps)
    def _(j):
        level, p = order(j)
        for kind in range(2):
            @pl.when(sends_up(level))
            def _():
                up_copy(level, kind, p).wait_send()

            @pl.when(sends_down(level))
            def _():
                down_copy(level, kind, p).wait_send()

            for i in range(1, nb):
                side_copy(i, level, kind, p).wait_send()
            for bb in range(nb):
                core_copy(bb, level, kind, p).wait_send()

    @pl.loop(1, n_rows)
    def _(j):
        stat_copy(j, lax.rem(r + j, n_rows)).wait_recv()

    all_high = stat[:, 0, :]
    all_sum = stat[:, 1, :]
    highest = jnp.max(all_high, axis=0, keepdims=True)
    column_sum = jnp.sum(all_sum * jnp.exp(all_high - highest), axis=0, keepdims=True)
    pot_ref[...] = jnp.log(mass_ref[...]) - highest - jnp.log(column_sum)
    scale = total * mass_ref[...] / column_sum

    @pl.loop(0, CHUNKS)
    def _(c):
        rows = pl.ds(pl.multiple_of(c * mc, mc), mc)
        factor = jnp.exp(cmax[c, 0:1, :] - highest) * scale
        trans_ref[rows, :] = (acc[rows, 0:half] * factor).astype(trans_ref.dtype)

    @pl.loop(1, n_rows)
    def _(j):
        stat_copy(j, r).wait_send()


def body(n_rows, total, dist_first, coupling, dist_second, row_potential, column_cost, column_mass):
    m, width = dist_first.shape
    kc = coupling.shape[1]
    depth, half = dist_second.shape
    nb = n_rows // (2 * LEVELS)
    block = width // (2 * SUBS)
    vmem = pl.BlockSpec(memory_space=pltpu.VMEM)
    hbm = pl.BlockSpec(memory_space=pl.ANY)
    dma = pltpu.SemaphoreType.DMA
    transport, potential = pl.pallas_call(
        functools.partial(kernel, n_rows, width, float(total)),
        out_shape=(
            jax.ShapeDtypeStruct((m, half), jnp.bfloat16),
            jax.ShapeDtypeStruct((1, half), jnp.float32),
        ),
        in_specs=[hbm, vmem, vmem, vmem, vmem, vmem],
        out_specs=(vmem, vmem),
        scratch_shapes=[
            pltpu.VMEM((width, depth), jnp.bfloat16),
            pltpu.VMEM((depth, 2 * half), jnp.bfloat16),
            pltpu.VMEM((2, m, block), jnp.bfloat16),
            pltpu.VMEM((block, 2 * half), jnp.bfloat16),
            pltpu.VMEM((m, 2 * half), jnp.float32),
            pltpu.VMEM((m, 128), jnp.float32),
            pltpu.VMEM((m, half), SEND),
            pltpu.VMEM((m, half), SEND),
            pltpu.VMEM((n_rows, 8, half), jnp.float32),
            pltpu.VMEM((CHUNKS, 8, half), jnp.float32),
            dma((2, 2 * nb)),
            dma((2,)),
            dma((SUBS,)),
            dma((2, 2, 2, SUBS)),
            dma((nb, 2, 2, SUBS)),
            dma((nb, 2, 2, SUBS)),
            dma((2, nb, 2, 2, SUBS)),
            dma, dma,
            dma((CHUNKS,)), dma((CHUNKS,)),
            dma((n_rows,)), dma((n_rows,)),
        ],
        compiler_params=pltpu.CompilerParams(
            collective_id=0, has_side_effects=True, vmem_limit_bytes=60 * 1024 * 1024
        ),
        cost_estimate=pl.CostEstimate(
            flops=2 * m * width * 2 * half + 2 * width * depth * 2 * half,
            bytes_accessed=m * width * 2, transcendentals=m * half,
        ),
    )(
        dist_first, coupling, dist_second,
        row_potential.reshape(m // 128, 128),
        column_cost.reshape(1, half), column_mass.reshape(1, half),
    )
    return transport, potential.reshape(half)


def solution(mesh):
    n_rows = mesh.shape["row"]

    def run(dist_first, *rest):
        in_specs = (P("row", "col"), P("row", "col"), P(None, "col"), P("row"), P("col"), P("col"))
        out_specs = (P("row", "col"), P("col"))
        return jax.shard_map(
            functools.partial(body, n_rows, dist_first.shape[0]),
            mesh=mesh, in_specs=in_specs, out_specs=out_specs, check_vma=False,
        )(dist_first, *rest)

    return run
```
